1024 devices in a mesh: group: 32 (over y, x_lo, core), table: 16 (over z), batch: 2 (over x_hi).
Axes of the slice: x: 4 (x_hi: 2, x_lo: 2; x = x_hi * 2 + x_lo), y: 8, z: 16, core: 2. Of those that a mesh axis runs over, the one named last changes fastest.
Arguments:
- features_in: bfloat16 [64, 2048, 3456], P(('group', 'batch'), 'table'), may hold values from -6 to 6
- cross_cot: bfloat16 [64, 2048, 3456], P(('group', 'batch'), 'table'), may hold values from -6 to 6
- cross_down: bfloat16 [3456, 512], replicated, may hold values from -0.109375 to 0.109375
- cross_up: bfloat16 [512, 3456], replicated, may hold values from -0.25 to 0.25
- cross_bias: float32 [3456], replicated, may hold values from -3 to 3
- lookups: int32 [16, 64, 2048, 2], P('table', ('group', 'batch')), may hold values from 0 to 8191, as said below
Outputs:
- bottom_grad: bfloat16 [64, 2048, 128], P(('group', 'batch'), 'table')
- bias_grad: float32 [3456], replicated
- row_grad: float32 [16, 8192, 128], P('table', ('group', 'batch'))
The draws below stay inside these ranges and needn't reach their ends.
Inputs may be any that keep to these rules, and one draw needn't show every extreme that they name: Block b owns rows b * 128 to (b + 1) * 128 - 1 of each table. In each feature, the 4096 lookups of one block fall on the rows of any one block at most 96 times, and in each feature one block's rows receive exactly 96 lookups from every block.
All inputs are finite; a program needn't handle non-finite values.
Results may differ from the reference program's by a relative error of at most 0.012.
Values may be sent and summed in bfloat16 or wider, within the bound.
A program may use at most 64 MiB of HBM per device.

```python
import jax
import jax.numpy as jnp
from jax import lax

EMB = 128
BOTTOM = 128
RANK = 512
ROWS_DEV = 128
POOL = 2
WIDTH = 3456
FEATS = 16
BLOCKS = 64
TSAMP = 2048
ROWS = 8192
CAP = 96


def draw_lookups(key, part):
    key = jax.random.fold_in(key, 11)
    total = TSAMP * POOL

    def one_feature(feature_key):
        pick_key, block_key = jax.random.split(feature_key)
        fullest = jax.random.randint(pick_key, (), 0, BLOCKS)

        def one_block(single_key):
            first, second, third = jax.random.split(single_key, 3)
            others = jax.random.permutation(first, (BLOCKS - 1) * CAP)[:total - CAP] // CAP
            others = others + (others >= fullest).astype(jnp.int32)
            owners = jnp.concatenate([jnp.full((CAP,), fullest, jnp.int32), others.astype(jnp.int32)])
            owners = jax.random.permutation(second, owners)
            inner = jax.random.randint(third, (total,), 0, ROWS_DEV)
            return (owners * ROWS_DEV + inner).reshape(TSAMP, POOL)
        return jax.vmap(one_block)(jax.random.split(block_key, BLOCKS))
    return jax.vmap(one_feature)(jax.random.split(key, FEATS)).astype(jnp.int32)


def level_of(stream_key, shape, cuts, least, high):
    factor_of = 1.0
    for position, parts in cuts:
        heights = jax.random.uniform(jax.random.fold_in(jax.random.fold_in(stream_key, 6), position), (parts,), jnp.float32, least / len(cuts), high / len(cuts))
        factor_of = factor_of * jnp.repeat(jnp.exp(heights), shape[position] // parts).reshape((-1,) + (1,) * (len(shape) - 1 - position))
    return factor_of


def bell_draw(key, dims, scale, limit, cuts=(), kind=jnp.bfloat16):
    factor_of = level_of(key, dims, cuts, -0.22, 0.18) if cuts else 1.0
    result = jax.random.normal(key, dims, jnp.float32) * scale * factor_of
    return jnp.minimum(jnp.maximum(result, -limit), limit).astype(kind)


def setup_inputs(seed: int = 0) -> dict:
    streams_of = jax.random.split(jax.random.key(seed), 7)
    features_in = bell_draw(streams_of[0], (BLOCKS, TSAMP, WIDTH), 1.0, 6.0, ((0, 64), (1, 16)))
    cross_cot = bell_draw(streams_of[1], (BLOCKS, TSAMP, WIDTH), 1.0, 6.0, ((0, 64), (1, 16)))
    cross_down = bell_draw(streams_of[2], (WIDTH, RANK), WIDTH ** -0.5, 0.109375)
    cross_up = bell_draw(streams_of[3], (RANK, WIDTH), RANK ** -0.5, 0.25)
    cross_bias = bell_draw(streams_of[4], (WIDTH,), 0.5, 3.0, (), jnp.float32)
    lookups = draw_lookups(jax.random.fold_in(streams_of[6], 71), 0)
    return {"features_in": features_in, "cross_cot": cross_cot, "cross_down": cross_down, "cross_up": cross_up, "cross_bias": cross_bias, "lookups": lookups}


def reference(features_in, cross_cot, cross_down, cross_up, cross_bias, lookups):
    def one_block(pair):
        inputs, cotan = pair
        low = jnp.dot(inputs, cross_down, preferred_element_type=jnp.float32).astype(jnp.bfloat16)
        gate = jnp.dot(low, cross_up, preferred_element_type=jnp.float32) + cross_bias
        cot_wide = cotan.astype(jnp.float32)
        gate_grad = cot_wide * inputs.astype(jnp.float32)
        low_grad = jnp.dot(gate_grad.astype(jnp.bfloat16), cross_up.T, preferred_element_type=jnp.float32).astype(jnp.bfloat16)
        input_grad = (cot_wide * (gate + 1.0) + jnp.dot(low_grad, cross_down.T, preferred_element_type=jnp.float32)).astype(jnp.bfloat16)
        pooled = input_grad[:, BOTTOM:BOTTOM + FEATS * EMB].reshape(-1, FEATS, EMB)
        return input_grad[:, :BOTTOM], pooled, jnp.sum(gate_grad, 0)

    bottom_grad, pooled, partial_value = lax.map(one_block, (features_in, cross_cot))
    bias_grad = jnp.sum(partial_value, 0)

    def table_rows(feature):
        values = lax.dynamic_index_in_dim(pooled, feature, 2, keepdims=False).astype(jnp.float32)
        spread = jnp.broadcast_to(values[:, :, None, :], (BLOCKS, TSAMP, POOL, EMB)).reshape(-1, EMB)
        row_ids = lax.dynamic_index_in_dim(lookups, feature, 0, keepdims=False).reshape(-1)
        return jax.ops.segment_sum(spread, row_ids, num_segments=ROWS)

    row_grad = lax.map(table_rows, jnp.arange(FEATS, dtype=jnp.int32))
    return bottom_grad, bias_grad, row_grad
```

```python
import functools

import jax
import jax.numpy as jnp
from jax import lax
from jax.experimental import pallas as pl
from jax.experimental.pallas import tpu as pltpu
from jax.sharding import PartitionSpec as P

MESH = pl.DeviceIdType.MESH
F32 = jnp.float32
BF16 = jnp.bfloat16
EMB = 128
ROWS_DEV = 128
XLO = 2
CORES = 2
KCHUNK = 384


def offset_of(step, size):
    half = (step + 1) // 2
    odd = step % 2
    return size // 2 + half * (1 - 2 * odd)


def kernel(
    sizes,
    feat_hbm, cot_hbm, down_hbm, up_hbm, bias_ref, ids_ref,
    bottom_ref, bias_out, row_out,
    feat, cot, down, up, low, low_grad, low_acc, grad_acc,
    pooled, vals, ids, hi, lo, acc,
    xs, xr, ys, yr,
    bias_part, bias_z, bias_c, bias_x, bias_y, bias_all,
    load_sem, ids_sem, zs_sem, zr_sem, fs_sem, fr_sem, xs_sem, xr_sem, ys_sem, yr_sem,
    bzs_sem, bzr_sem, bc_sem, bxs_sem, bxr_sem, bys_sem, byr_sem, bas_sem, bar_sem,
):
    ny, nx, nz = sizes
    width = feat.shape[1]
    chunks = width // KCHUNK
    group = lax.axis_index("group")
    x_hi = lax.axis_index("batch")
    z = lax.axis_index("table")
    y = group // (XLO * CORES)
    x_lo = (group // CORES) % XLO
    core = group % CORES
    x = x_hi * XLO + x_lo

    def device(xx, yy, zz, cc):
        return {"group": (yy * XLO + xx % XLO) * CORES + cc, "table": zz, "batch": xx // XLO}

    sibling = device(x, y, z, 1 - core)

    def x_peer(offset):
        return device((x + offset) % nx, y, z, core)

    def y_peer(offset):
        return device(x, (y + offset) % ny, z, core)

    def z_peer(offset):
        return device(x, y, (z + offset) % nz, core)

    def remote(src, dst, send, recv, target):
        return pltpu.make_async_remote_copy(
            src_ref=src, dst_ref=dst, send_sem=send, recv_sem=recv, device_id=target, device_id_type=MESH
        )

    barrier = pltpu.get_barrier_semaphore()

    def greet(target):
        pl.semaphore_signal(barrier, inc=1, device_id=target, device_id_type=MESH)

    greet(sibling)
    lax.fori_loop(1, nx, lambda i, c: (greet(x_peer(i)), c)[1], 0)
    lax.fori_loop(1, ny, lambda i, c: (greet(y_peer(i)), c)[1], 0)
    lax.fori_loop(1, nz, lambda i, c: (greet(z_peer(i)), c)[1], 0)

    def loads(k):
        cols = pl.ds(k * KCHUNK, KCHUNK)
        return (
            pltpu.make_async_copy(feat_hbm.at[:, cols], feat.at[:, cols], load_sem.at[0, k]),
            pltpu.make_async_copy(cot_hbm.at[:, cols], cot.at[:, cols], load_sem.at[1, k]),
            pltpu.make_async_copy(down_hbm.at[cols, :], down.at[cols, :], load_sem.at[2, k]),
            pltpu.make_async_copy(up_hbm.at[:, cols], up.at[:, cols], load_sem.at[3, k]),
        )

    for k in range(chunks):
        for copy in loads(k):
            copy.start()

    acc[...] = jnp.zeros_like(acc)
    bias_part[...] = jnp.zeros_like(bias_part)

    for k in range(chunks):
        for copy in loads(k):
            copy.wait()
        cols = slice(k * KCHUNK, (k + 1) * KCHUNK)
        part_in = feat[:, cols]
        gate_grad = cot[:, cols].astype(F32) * part_in.astype(F32)
        sums = jnp.sum(gate_grad, 0, keepdims=True)
        for j in range(KCHUNK // 128):
            g = k * (KCHUNK // 128) + j
            bias_part[g // 2, g % 2 : g % 2 + 1, :] = sums[:, j * 128 : (j + 1) * 128]
        first = jnp.dot(part_in, down[cols, :], preferred_element_type=F32)
        second = lax.dot_general(
            gate_grad.astype(BF16), up[:, cols], (((1,), (1,)), ((), ())), preferred_element_type=F32
        )
        if k == 0:
            low_acc[...] = first
            grad_acc[...] = second
        else:
            low_acc[...] += first
            grad_acc[...] += second
    low[...] = low_acc[...].astype(BF16)
    low_grad[...] = grad_acc[...].astype(BF16)

    pl.semaphore_wait(barrier, 1 + (nx - 1) + (ny - 1) + (nz - 1))

    ids_copy = remote(ids_ref, ids.at[core], ids_sem.at[0], ids_sem.at[1], sibling)
    ids_copy.start()
    ids[core] = ids_ref[...]

    def columns(start):
        cols = pl.ds(pl.multiple_of(start, 128), 128)
        gate = jnp.dot(low[...], up[:, cols], preferred_element_type=F32) + bias_ref[:, cols]
        back = lax.dot_general(
            low_grad[...], down[cols, :], (((1,), (1,)), ((), ())), preferred_element_type=F32
        )
        return (cot[:, cols].astype(F32) * (gate + 1.0) + back).astype(BF16)

    mine = pl.ds(pl.multiple_of(core * 128, 128), 128)

    def z_copy(step):
        offset = offset_of(step, nz)
        return remote(
            pooled.at[step], vals.at[z, mine], zs_sem.at[step], zr_sem.at[z], z_peer(offset)
        )

    def z_arrival(source):
        return remote(pooled.at[0], vals.at[source, mine], zs_sem.at[0], zr_sem.at[source], sibling)

    def bias_z_copy(step):
        offset = offset_of(step, nz)
        return remote(
            bias_part.at[(z + offset) % nz], bias_z.at[z], bzs_sem.at[step], bzr_sem.at[z], z_peer(offset)
        )

    def send_feature(step, carry):
        feature = (z + offset_of(step, nz)) % nz
        pooled[step] = columns(128 + feature * 128)
        z_copy(step).start()
        bias_z_copy(step).start()
        return carry

    send_feature(0, 0)

    def send_two(pair, carry):
        send_feature(2 * pair + 1, carry)
        send_feature(2 * pair + 2, carry)
        return carry

    lax.fori_loop(0, nz // 2 - 1, send_two, 0)
    vals[z, mine] = columns(128 + z * 128)

    def forward(source):
        place = vals.at[source, mine]
        return remote(place, place, fs_sem.at[source], fr_sem.at[source], sibling)

    def forwarded(source):
        place = vals.at[source, pl.ds(pl.multiple_of((1 - core) * 128, 128), 128)]
        return remote(place, place, fs_sem.at[source], fr_sem.at[source], sibling)

    forward(z).start()
    bottom_ref[...] = columns(0)

    remote(ids_ref, ids.at[1 - core], ids_sem.at[0], ids_sem.at[1], sibling).wait_recv()

    def split_ids(zz, carry):
        part = pl.ds(pl.multiple_of(zz * 128, 128), 128)
        for c in range(CORES):
            row = ids[c, :, part]
            block = row >> 7
            xx = (block & 1) * XLO + ((block >> 2) & 1)
            tile = xx * ny + (block >> 3)
            hi[zz, :, c * 128 : (c + 1) * 128] = jnp.where(((block >> 1) & 1) == core, tile, -1)
            lo[zz, :, c * 128 : (c + 1) * 128] = row & 127
        return carry

    lax.fori_loop(0, nz, split_ids, 0)

    def add_rows(source):
        value = vals[source]
        tile_of, inner = hi[source], lo[source]
        rows = lax.broadcasted_iota(jnp.int32, (ROWS_DEV, 256), 0).astype(F32).astype(BF16)
        one, zero = jnp.ones((), BF16), jnp.zeros((), BF16)
        for t in range(nx * ny):
            hit = jnp.where(tile_of == t, inner, -1).astype(F32).astype(BF16)
            onehot = jnp.where(rows == hit[0:1], one, zero) + jnp.where(rows == hit[1:2], one, zero)
            acc[t * 128 : (t + 1) * 128, :] += jnp.dot(onehot, value, preferred_element_type=F32)

    def source_of(step):
        return (z + nz - offset_of(step, nz)) % nz

    def arrive(step, carry):
        source = source_of(step)
        z_arrival(source).wait_recv()
        forward(source).start()
        before = (z + nz - offset_of((step + nz - 1) % nz, nz)) % nz
        forwarded(before).wait_recv()
        add_rows(before)
        return carry

    lax.fori_loop(0, nz - 1, arrive, 0)
    last = source_of(nz - 2)
    forwarded(last).wait_recv()
    add_rows(last)

    def tile_at(xx, yy):
        return acc[pl.ds(pl.multiple_of((xx * ny + yy) * 128, 128), 128), :]

    def x_copy(j, i):
        return remote(
            xs.at[j, i], xr.at[j, i], xs_sem.at[j, i], xr_sem.at[j, i], x_peer(offset_of(i, nx))
        )

    def send_x(j, carry):
        yy = (y + offset_of(j, ny)) % ny
        for i in range(nx - 1):
            xs[j, i] = tile_at((x + offset_of(i, nx)) % nx, yy).astype(BF16)
            x_copy(j, i).start()
        return carry

    lax.fori_loop(0, ny, send_x, 0)

    def bias_z_wait(step, carry):
        source = source_of(step)
        remote(bias_part.at[0], bias_z.at[source], bzs_sem.at[0], bzr_sem.at[source], sibling).wait_recv()
        return carry

    lax.fori_loop(0, nz - 1, bias_z_wait, 0)
    bias_z[z] = bias_part[z]
    bias_c[core] = jnp.sum(bias_z[...], 0)
    c_copy = remote(bias_c.at[core], bias_c.at[core], bc_sem.at[0], bc_sem.at[1], sibling)
    c_copy.start()

    def y_copy(j):
        return remote(ys.at[j], yr.at[j], ys_sem.at[j], yr_sem.at[j], y_peer(offset_of(j, ny)))

    def sum_x(j):
        yy = (y + offset_of(j, ny)) % ny
        total = tile_at(x, yy)
        for i in range(nx - 1):
            x_copy(j, i).wait_recv()
            total += xr[j, i].astype(F32)
        return total

    def send_y(j, carry):
        ys[j] = sum_x(j).astype(BF16)
        y_copy(j).start()
        return carry

    def bx_copy(i):
        return remote(bias_x.at[x], bias_x.at[x], bxs_sem.at[i], bxr_sem.at[x], x_peer(offset_of(i, nx)))

    def by_copy(j):
        return remote(bias_y.at[y], bias_y.at[y], bys_sem.at[j], byr_sem.at[y], y_peer(offset_of(j, ny)))

    def ba_copy(step):
        return remote(
            bias_all.at[z], bias_all.at[z], bas_sem.at[step], bar_sem.at[z], z_peer(offset_of(step, nz))
        )

    cut = [(ny - 1) * q // 4 for q in range(5)]
    lax.fori_loop(cut[0], cut[1], send_y, 0)

    remote(bias_c.at[core], bias_c.at[1 - core], bc_sem.at[0], bc_sem.at[1], sibling).wait_recv()
    bias_x[x] = bias_c[0] + bias_c[1]
    for i in range(nx - 1):
        bx_copy(i).start()

    lax.fori_loop(cut[1], cut[2], send_y, 0)

    for i in range(nx - 1):
        source = (x + nx - offset_of(i, nx)) % nx
        remote(bias_x.at[x], bias_x.at[source], bxs_sem.at[i], bxr_sem.at[source], sibling).wait_recv()
    bias_y[y] = jnp.sum(bias_x[...], 0)
    lax.fori_loop(0, ny - 1, lambda j, c: (by_copy(j).start(), c)[1], 0)

    lax.fori_loop(cut[2], cut[3], send_y, 0)

    def by_wait(j, carry):
        source = (y + ny - offset_of(j, ny)) % ny
        remote(bias_y.at[y], bias_y.at[source], bys_sem.at[j], byr_sem.at[source], sibling).wait_recv()
        return carry

    lax.fori_loop(0, ny - 1, by_wait, 0)
    bias_all[z] = jnp.sum(bias_y[...], 0)
    lax.fori_loop(0, nz - 1, lambda s, c: (ba_copy(s).start(), c)[1], 0)

    lax.fori_loop(cut[3], cut[4], send_y, 0)

    total = sum_x(ny - 1)
    for j in range(ny - 1):
        y_copy(j).wait_recv()
        total += yr[j].astype(F32)
    row_out[...] = total

    def ba_wait(step, carry):
        source = source_of(step)
        remote(bias_all.at[z], bias_all.at[source], bas_sem.at[0], bar_sem.at[source], sibling).wait_recv()
        return carry

    lax.fori_loop(0, nz - 1, ba_wait, 0)
    for g in range(width // 128):
        bias_out[g : g + 1, :] = bias_all[g // 2, g % 2 : g % 2 + 1, :]

    ids_copy.wait_send()
    c_copy.wait_send()

    def sent_z(step, carry):
        z_copy(step).wait_send()
        bias_z_copy(step).wait_send()
        ba_copy(step).wait_send()
        return carry

    lax.fori_loop(0, nz - 1, sent_z, 0)
    lax.fori_loop(0, nz, lambda s, c: (forward(s).wait_send(), c)[1], 0)

    def sent_y(j, carry):
        y_copy(j).wait_send()
        by_copy(j).wait_send()
        return carry

    lax.fori_loop(0, ny - 1, sent_y, 0)

    def sent_x(j, carry):
        for i in range(nx - 1):
            x_copy(j, i).wait_send()
        return carry

    lax.fori_loop(0, ny, sent_x, 0)
    for i in range(nx - 1):
        bx_copy(i).wait_send()


def body(sizes, features_in, cross_cot, cross_down, cross_up, cross_bias, lookups):
    ny, nx, nz = sizes
    samples, width = features_in.shape[1:]
    rank = cross_down.shape[1]
    tsamp = lookups.shape[2]
    vmem = pl.BlockSpec(memory_space=pltpu.VMEM)
    anywhere = pl.BlockSpec(memory_space=pl.ANY)
    dma = pltpu.SemaphoreType.DMA
    tile = (8, 128)
    bottom, bias, rows = pl.pallas_call(
        functools.partial(kernel, sizes),
        out_shape=(
            jax.ShapeDtypeStruct((samples, EMB), BF16),
            jax.ShapeDtypeStruct((width // 128, 128), F32),
            jax.ShapeDtypeStruct((ROWS_DEV, EMB), F32),
        ),
        in_specs=[anywhere] * 4 + [vmem] * 2,
        out_specs=(vmem, vmem, vmem),
        scratch_shapes=[
            pltpu.VMEM((samples, width), BF16),
            pltpu.VMEM((samples, width), BF16),
            pltpu.VMEM((width, rank), BF16),
            pltpu.VMEM((rank, width), BF16),
            pltpu.VMEM((samples, rank), BF16),
            pltpu.VMEM((samples, rank), BF16),
            pltpu.VMEM((samples, rank), F32),
            pltpu.VMEM((samples, rank), F32),
            pltpu.VMEM((nz - 1, samples, EMB), BF16),
            pltpu.VMEM((nz, 2 * samples, EMB), BF16),
            pltpu.VMEM((CORES, 2, tsamp), jnp.int32),
            pltpu.VMEM((nz, 2, 256), jnp.int32),
            pltpu.VMEM((nz, 2, 256), jnp.int32),
            pltpu.VMEM((nx * ny * ROWS_DEV, EMB), F32),
            pltpu.VMEM((ny, nx - 1, ROWS_DEV, EMB), BF16),
            pltpu.VMEM((ny, nx - 1, ROWS_DEV, EMB), BF16),
            pltpu.VMEM((ny - 1, ROWS_DEV, EMB), BF16),
            pltpu.VMEM((ny - 1, ROWS_DEV, EMB), BF16),
            pltpu.VMEM((nz,) + tile, F32),
            pltpu.VMEM((nz,) + tile, F32),
            pltpu.VMEM((CORES,) + tile, F32),
            pltpu.VMEM((nx,) + tile, F32),
            pltpu.VMEM((ny,) + tile, F32),
            pltpu.VMEM((nz,) + tile, F32),
            dma((4, width // KCHUNK)),
            dma((2,)),
            dma((nz - 1,)),
            dma((nz,)),
            dma((nz,)),
            dma((nz,)),
            dma((ny, nx - 1)),
            dma((ny, nx - 1)),
            dma((ny - 1,)),
            dma((ny - 1,)),
            dma((nz - 1,)),
            dma((nz,)),
            dma((2,)),
            dma((nx - 1,)),
            dma((nx,)),
            dma((ny - 1,)),
            dma((ny,)),
            dma((nz - 1,)),
            dma((nz,)),
        ],
        compiler_params=pltpu.CompilerParams(
            collective_id=0, has_side_effects=True, vmem_limit_bytes=40 << 20
        ),
        name="cross_backward",
    )(
        features_in[0],
        cross_cot[0],
        cross_down,
        cross_up,
        cross_bias.reshape(1, width),
        lookups[0, 0].T,
    )
    return bottom[None], bias.reshape(width), rows[None]


def solution(mesh):
    sizes = (
        mesh.shape["group"] // (XLO * CORES),
        XLO * mesh.shape["batch"],
        mesh.shape["table"],
    )
    placed = (
        P(("group", "batch"), "table", None),
        P(("group", "batch"), "table", None),
        P(),
        P(),
        P(),
        P("table", ("group", "batch"), None, None),
    )
    return jax.shard_map(
        functools.partial(body, sizes),
        mesh=mesh,
        in_specs=placed,
        out_specs=(P(("group", "batch"), "table", None), P(), P("table", ("group", "batch"), None)),
        check_vma=False,
    )
```

```python
import functools

import jax
import jax.numpy as jnp
from jax import lax
from jax.experimental import pallas as pl
from jax.experimental.pallas import tpu as pltpu
from jax.sharding import PartitionSpec as P

MESH = pl.DeviceIdType.MESH
F32 = jnp.float32
BF16 = jnp.bfloat16
EMB = 128
ROWS_DEV = 128
XLO = 2
CORES = 2
CUTS = (8, 10, 12, 15)
XLAG = 3
CLAG = 5
KCHUNK = 1152


def offset_of(step, size):
    half = (step + 1) // 2
    odd = step % 2
    return size // 2 + half * (1 - 2 * odd)


def near_of(step, size):
    return offset_of((2 * size - 2 - step) % size, size)


def kernel(
    sizes,
    feat_hbm, cot_hbm, down_hbm, up_hbm, bias_hbm, ids_hbm,
    bottom_ref, bias_out, row_out,
    feat, cot, down, up, bias, low, low_grad, low_acc, grad_acc,
    pooled, vals, ids, tile_of, inner, acc, ys, yr,
    bias_part, bias_z, bias_c, bias_x, bias_y, bias_all,
    load_sem, id_sem, idr_sem, zs_sem, zr_sem, xs_sem, xr_sem, fs_sem, fr_sem, ys_sem, yr_sem,
    bzs_sem, bzr_sem, bc_sem, bxs_sem, bxr_sem, bys_sem, byr_sem, bas_sem, bar_sem,
):
    ny, nx, nz = sizes
    width = feat.shape[1]
    chunks = width // KCHUNK
    group = lax.axis_index("group")
    x_hi = lax.axis_index("batch")
    z = lax.axis_index("table")
    y = group // (XLO * CORES)
    x_lo = (group // CORES) % XLO
    core = group % CORES
    x = x_hi * XLO + x_lo

    def device(xx, yy, zz, cc):
        return {"group": (yy * XLO + xx % XLO) * CORES + cc, "table": zz, "batch": xx // XLO}

    sibling = device(x, y, z, 1 - core)

    def x_peer(offset):
        return device((x + offset) % nx, y, z, core)

    def y_peer(offset):
        return device(x, (y + offset) % ny, z, core)

    def z_peer(offset):
        return device(x, y, (z + offset) % nz, core)

    def remote(src, dst, send, recv, target):
        return pltpu.make_async_remote_copy(
            src_ref=src, dst_ref=dst, send_sem=send, recv_sem=recv, device_id=target, device_id_type=MESH
        )

    def each(count, act):
        lax.fori_loop(0, count, lambda i, c: (act(i), c)[1], 0)

    def loads(k):
        cols = pl.ds(k * KCHUNK, KCHUNK)
        return (
            pltpu.make_async_copy(feat_hbm.at[:, cols], feat.at[:, cols], load_sem.at[0, k]),
            pltpu.make_async_copy(cot_hbm.at[:, cols], cot.at[:, cols], load_sem.at[1, k]),
            pltpu.make_async_copy(down_hbm.at[cols, :], down.at[cols, :], load_sem.at[2, k]),
            pltpu.make_async_copy(up_hbm.at[:, cols], up.at[:, cols], load_sem.at[3, k]),
        )

    for k in range(chunks):
        for copy in loads(k):
            copy.start()
    place = core * nx + x
    load_bias = pltpu.make_async_copy(bias_hbm, bias, load_sem.at[0, chunks])
    load_ids = pltpu.make_async_copy(ids_hbm, ids.at[place], load_sem.at[1, chunks])
    load_bias.start()
    load_ids.start()

    barrier = pltpu.get_barrier_semaphore()

    def greet(target):
        pl.semaphore_signal(barrier, inc=1, device_id=target, device_id_type=MESH)

    each(nz - 1, lambda i: greet(z_peer(offset_of(i, nz))))
    each(ny - 1, lambda i: greet(y_peer(offset_of(i, ny))))
    for offset in range(1, nx):
        greet(x_peer(offset))
        greet(device((x + offset) % nx, y, z, 1 - core))
    greet(sibling)

    acc[...] = jnp.zeros_like(acc)
    bias_part[...] = jnp.zeros_like(bias_part)

    for k in range(chunks):
        for copy in loads(k):
            copy.wait()
        cols = slice(k * KCHUNK, (k + 1) * KCHUNK)
        part_in = feat[:, cols]
        gate_grad = cot[:, cols].astype(F32) * part_in.astype(F32)
        sums = jnp.sum(gate_grad, 0, keepdims=True)
        for j in range(KCHUNK // 128):
            g = k * (KCHUNK // 128) + j
            bias_part[g // 2, g % 2 : g % 2 + 1, :] = sums[:, j * 128 : (j + 1) * 128]
        first = jnp.dot(part_in, down[cols, :], preferred_element_type=F32)
        second = lax.dot_general(
            gate_grad.astype(BF16), up[:, cols], (((1,), (1,)), ((), ())), preferred_element_type=F32
        )
        if k == 0:
            low_acc[...] = first
            grad_acc[...] = second
        else:
            low_acc[...] += first
            grad_acc[...] += second
    low[...] = low_acc[...].astype(BF16)
    low_grad[...] = grad_acc[...].astype(BF16)
    load_bias.wait()
    load_ids.wait()

    def columns(start, count):
        cols = slice(start, start + count)
        gate = jnp.dot(low[...], up[:, cols], preferred_element_type=F32) + bias[cols].reshape(1, count)
        back = lax.dot_general(
            low_grad[...], down[cols, :], (((1,), (1,)), ((), ())), preferred_element_type=F32
        )
        return (cot[:, cols].astype(F32) * (gate + 1.0) + back).astype(BF16)

    for f in range(0, nz, 2):
        pair = columns(128 + f * 128, 256)
        pooled[f] = pair[:, :128]
        pooled[f + 1] = pair[:, 128:]

    pl.semaphore_wait(barrier, (nz - 1) + (ny - 1) + 2 * (nx - 1) + 1)

    def bias_z_copy(step):
        offset = near_of(step, nz)
        return remote(
            bias_part.at[(z + offset) % nz], bias_z.at[z], bzs_sem.at[step], bzr_sem.at[z], z_peer(offset)
        )

    each(nz - 1, lambda s: bias_z_copy(s).start())

    mine = pl.ds(pl.multiple_of(x * 128, 128), 128)

    def z_copy(step):
        offset = near_of(step, nz)
        return remote(
            pooled.at[(z + offset) % nz], vals.at[z, core, mine], zs_sem.at[step], zr_sem.at[z], z_peer(offset)
        )

    each(nz - 1, lambda s: z_copy(s).start())

    def id_copy(i):
        if i == nx - 1:
            target = sibling
        elif i < nx - 1:
            target = x_peer(i + 1)
        else:
            target = device((x + i - nx + 1) % nx, y, z, 1 - core)
        return remote(ids.at[place], ids.at[place], id_sem.at[i], idr_sem.at[place], target)

    for i in range(2 * nx - 1):
        id_copy(i).start()

    vals[z, core, mine] = pooled[z]

    def source_of(step):
        return (z + nz - near_of(step, nz)) % nz

    def z_wait(source):
        remote(pooled.at[0], vals.at[source, core, mine], zs_sem.at[0], zr_sem.at[source], sibling).wait_recv()

    def x_copy(source, i):
        spot = vals.at[source, core, mine]
        return remote(spot, spot, xs_sem.at[source, i], xr_sem.at[source, x], x_peer(offset_of(i, nx)))

    def x_send(source):
        for i in range(nx - 1):
            x_copy(source, i).start()

    def x_wait(source):
        for i in range(nx - 1):
            there = (x + nx - offset_of(i, nx)) % nx
            spot = vals.at[source, core, pl.ds(pl.multiple_of(there * 128, 128), 128)]
            remote(spot, spot, xs_sem.at[source, i], xr_sem.at[source, there], sibling).wait_recv()

    def core_copy(source):
        spot = vals.at[source, core]
        return remote(spot, spot, fs_sem.at[source], fr_sem.at[source], sibling)

    def core_wait(source):
        spot = vals.at[source, 1 - core]
        remote(spot, spot, fs_sem.at[source], fr_sem.at[source], sibling).wait_recv()

    x_send(z)

    bottom_ref[...] = columns(0, 128)

    for c in range(CORES):
        for xx in range(nx):
            k = c * nx + xx

            @pl.when(k != place)
            def _():
                remote(ids.at[k], ids.at[k], id_sem.at[0], idr_sem.at[k], sibling).wait_recv()

            row = ids[k]
            block = row >> 7
            here = (((block >> 1) & 1) == core) & ((block & 1) == x_hi) & (((block >> 2) & 1) == x_lo)
            tile_of[2 * k : 2 * k + 2, :] = jnp.where(here, block >> 3, -1)
            inner[2 * k : 2 * k + 2, :] = row & 127

    def products(source, tiles):
        part = pl.ds(pl.multiple_of(source * 128, 128), 128)
        tile_here, inner_here = tile_of[:, part], inner[:, part]
        value = vals[source].reshape(CORES * nx * 128, EMB)
        rows = lax.broadcasted_iota(jnp.int32, (ROWS_DEV, 128), 0).astype(F32).astype(BF16)
        one, zero = jnp.ones((), BF16), jnp.zeros((), BF16)
        for t in tiles:
            hit = jnp.where(tile_here == t, inner_here, -1).astype(F32).astype(BF16)
            onehot = jnp.concatenate(
                [
                    jnp.where(rows == hit[2 * k : 2 * k + 1], one, zero)
                    + jnp.where(rows == hit[2 * k + 1 : 2 * k + 2], one, zero)
                    for k in range(CORES * nx)
                ],
                1,
            )
            yield t, jnp.dot(onehot, value, preferred_element_type=F32)

    def add_rows(source):
        for t, product in products(source, range(ny)):
            acc[t * 128 : (t + 1) * 128, :] += product

    def nth(k):
        return source_of((k + nz - 1) % nz)

    def arrive(k):
        z_wait(nth(k))
        x_send(nth(k))

    def gather(k):
        x_wait(nth(k))
        core_copy(nth(k)).start()

    def add(k):
        core_wait(nth(k))
        add_rows(nth(k))

    def all_three(k, carry):
        arrive(k)
        gather(k - XLAG)
        add(k - CLAG)
        return carry

    for k in range(1, CLAG):
        arrive(k)
        if k >= XLAG:
            gather(k - XLAG)

    lax.fori_loop(CLAG, CUTS[0], all_three, 0)

    def bias_z_wait(step):
        source = source_of(step)
        remote(bias_part.at[0], bias_z.at[source], bzs_sem.at[0], bzr_sem.at[source], sibling).wait_recv()

    each(nz - 1, bias_z_wait)
    bias_z[z] = bias_part[z]
    bias_c[core] = jnp.sum(bias_z[...], 0)
    c_copy = remote(bias_c.at[core], bias_c.at[core], bc_sem.at[0], bc_sem.at[1], sibling)
    c_copy.start()

    lax.fori_loop(CUTS[0], CUTS[1], all_three, 0)

    def bx_copy(i):
        return remote(bias_x.at[x], bias_x.at[x], bxs_sem.at[i], bxr_sem.at[x], x_peer(offset_of(i, nx)))

    def by_copy(j):
        return remote(bias_y.at[y], bias_y.at[y], bys_sem.at[j], byr_sem.at[y], y_peer(offset_of(j, ny)))

    def ba_copy(step):
        return remote(
            bias_all.at[z], bias_all.at[z], bas_sem.at[step], bar_sem.at[z], z_peer(near_of(step, nz))
        )

    remote(bias_c.at[core], bias_c.at[1 - core], bc_sem.at[0], bc_sem.at[1], sibling).wait_recv()
    bias_x[x] = bias_c[0] + bias_c[1]
    for i in range(nx - 1):
        bx_copy(i).start()

    lax.fori_loop(CUTS[1], CUTS[2], all_three, 0)

    for i in range(nx - 1):
        source = (x + nx - offset_of(i, nx)) % nx
        remote(bias_x.at[x], bias_x.at[source], bxs_sem.at[i], bxr_sem.at[source], sibling).wait_recv()
    bias_y[y] = jnp.sum(bias_x[...], 0)
    each(ny - 1, lambda j: by_copy(j).start())

    lax.fori_loop(CUTS[2], CUTS[3], all_three, 0)

    def by_wait(j):
        source = (y + ny - offset_of(j, ny)) % ny
        remote(bias_y.at[y], bias_y.at[source], bys_sem.at[j], byr_sem.at[source], sibling).wait_recv()

    each(ny - 1, by_wait)
    bias_all[z] = jnp.sum(bias_y[...], 0)
    each(nz - 1, lambda s: ba_copy(s).start())

    lax.fori_loop(CUTS[3], nz, all_three, 0)

    for k in range(nz, nz + CLAG - 1):
        if k - XLAG < nz:
            gather(k - XLAG)
        add(k - CLAG)
    last = nth(nz - 1)
    core_wait(last)

    def y_copy(j):
        return remote(ys.at[j], yr.at[j], ys_sem.at[j], yr_sem.at[j], y_peer(offset_of(j, ny)))

    order = [(y + offset_of(j, ny)) % ny for j in range(ny)]
    total = None
    for j, (t, product) in enumerate(products(last, order)):
        whole = acc[pl.ds(pl.multiple_of(t * 128, 128), 128), :] + product
        if j < ny - 1:
            ys[j] = whole.astype(BF16)
            y_copy(j).start()
        else:
            total = whole

    for i in range(2 * nx - 1):
        id_copy(i).wait_send()
    c_copy.wait_send()
    for i in range(nx - 1):
        bx_copy(i).wait_send()
    each(ny - 1, lambda j: by_copy(j).wait_send())

    def sent_z(step):
        z_copy(step).wait_send()
        bias_z_copy(step).wait_send()

    def sent_block(source):
        for i in range(nx - 1):
            x_copy(source, i).wait_send()
        core_copy(source).wait_send()

    each(nz - 1, sent_z)
    each(nz, sent_block)

    def ba_wait(step):
        source = source_of(step)
        remote(bias_all.at[z], bias_all.at[source], bas_sem.at[0], bar_sem.at[source], sibling).wait_recv()
        ba_copy(step).wait_send()

    each(nz - 1, ba_wait)
    for g in range(width // 128):
        bias_out[g : g + 1, :] = bias_all[g // 2, g % 2 : g % 2 + 1, :]

    for j in range(ny - 1):
        y_copy(j).wait_recv()
        total += yr[j].astype(F32)
    row_out[...] = total
    each(ny - 1, lambda j: y_copy(j).wait_send())


def body(sizes, features_in, cross_cot, cross_down, cross_up, cross_bias, lookups):
    ny, nx, nz = sizes
    samples, width = features_in.shape[1:]
    rank = cross_down.shape[1]
    tsamp = lookups.shape[2]
    group = CORES * nx
    vmem = pl.BlockSpec(memory_space=pltpu.VMEM)
    anywhere = pl.BlockSpec(memory_space=pl.ANY)
    dma = pltpu.SemaphoreType.DMA
    bottom, bias, rows = pl.pallas_call(
        functools.partial(kernel, sizes),
        out_shape=(
            jax.ShapeDtypeStruct((samples, EMB), BF16),
            jax.ShapeDtypeStruct((width // 128, 128), F32),
            jax.ShapeDtypeStruct((ROWS_DEV, EMB), F32),
        ),
        in_specs=[anywhere] * 6,
        out_specs=(vmem, vmem, vmem),
        scratch_shapes=[
            pltpu.VMEM((samples, width), BF16),
            pltpu.VMEM((samples, width), BF16),
            pltpu.VMEM((width, rank), BF16),
            pltpu.VMEM((rank, width), BF16),
            pltpu.VMEM((width,), F32),
            pltpu.VMEM((samples, rank), BF16),
            pltpu.VMEM((samples, rank), BF16),
            pltpu.VMEM((samples, rank), F32),
            pltpu.VMEM((samples, rank), F32),
            pltpu.VMEM((nz, samples, EMB), BF16),
            pltpu.VMEM((nz, CORES, nx * samples, EMB), BF16),
            pltpu.VMEM((group, 2, tsamp), jnp.int32),
            pltpu.VMEM((2 * group, tsamp), jnp.int32),
            pltpu.VMEM((2 * group, tsamp), jnp.int32),
            pltpu.VMEM((ny * ROWS_DEV, EMB), F32),
            pltpu.VMEM((ny - 1, ROWS_DEV, EMB), BF16),
            pltpu.VMEM((ny - 1, ROWS_DEV, EMB), BF16),
            pltpu.VMEM((nz, 2, 128), F32),
            pltpu.VMEM((nz, 2, 128), F32),
            pltpu.VMEM((CORES, 2, 128), F32),
            pltpu.VMEM((nx, 2, 128), F32),
            pltpu.VMEM((ny, 2, 128), F32),
            pltpu.VMEM((nz, 2, 128), F32),
            dma((4, width // KCHUNK + 1)),
            dma((2 * nx - 1,)),
            dma((2 * nx,)),
            dma((nz - 1,)),
            dma((nz,)),
            dma((nz, nx - 1)),
            dma((nz, nx)),
            dma((nz,)),
            dma((nz,)),
            dma((ny - 1,)),
            dma((ny - 1,)),
            dma((nz - 1,)),
            dma((nz,)),
            dma((2,)),
            dma((nx - 1,)),
            dma((nx,)),
            dma((ny - 1,)),
            dma((ny,)),
            dma((nz - 1,)),
            dma((nz,)),
        ],
        compiler_params=pltpu.CompilerParams(
            collective_id=0, has_side_effects=True, vmem_limit_bytes=62 << 20
        ),
        name="cross_backward",
    )(
        features_in[0],
        cross_cot[0],
        cross_down,
        cross_up,
        cross_bias,
        lookups[0, 0].T,
    )
    return bottom[None], bias.reshape(width), rows[None]


def solution(mesh):
    sizes = (
        mesh.shape["group"] // (XLO * CORES),
        XLO * mesh.shape["batch"],
        mesh.shape["table"],
    )
    placed = (
        P(("group", "batch"), "table", None),
        P(("group", "batch"), "table", None),
        P(),
        P(),
        P(),
        P("table", ("group", "batch"), None, None),
    )
    return jax.shard_map(
        functools.partial(body, sizes),
        mesh=mesh,
        in_specs=placed,
        out_specs=(P(("group", "batch"), "table", None), P(), P("table", ("group", "batch"), None)),
        check_vma=False,
    )
```

```python
import functools

import jax
import jax.numpy as jnp
from jax import lax
from jax.experimental import pallas as pl
from jax.experimental.pallas import tpu as pltpu
from jax.sharding import PartitionSpec as P

MESH = pl.DeviceIdType.MESH
F32 = jnp.float32
BF16 = jnp.bfloat16
EMB = 128
ROWS_DEV = 128
XLO = 2
CORES = 2
CUTS = (5, 6, 7, 9)
XLAG = 3
CLAG = 5
KCHUNK = 1152


def offset_of(step, size):
    half = (step + 1) // 2
    odd = step % 2
    return size // 2 + half * (1 - 2 * odd)


def near_of(step, size):
    return offset_of((2 * size - 2 - step) % size, size)


def kernel(
    sizes,
    feat_hbm, cot_hbm, down_hbm, up_hbm, bias_hbm, ids_hbm,
    bottom_ref, bias_out, row_out,
    feat, cot, down, up, bias, low, low_grad, low_acc, grad_acc,
    pooled, vals, ids, tile_of, inner, acc, ys, yr,
    bias_part, bias_z, bias_c, bias_x, bias_y, bias_all,
    load_sem, id_sem, idr_sem, zs_sem, zr_sem, xs_sem, xr_sem, fs_sem, fr_sem, ys_sem, yr_sem,
    bzs_sem, bzr_sem, bc_sem, bxs_sem, bxr_sem, bys_sem, byr_sem, bas_sem, bar_sem,
):
    ny, nx, nz = sizes
    width = feat.shape[1]
    chunks = width // KCHUNK
    group = lax.axis_index("group")
    x_hi = lax.axis_index("batch")
    z = lax.axis_index("table")
    y = group // (XLO * CORES)
    x_lo = (group // CORES) % XLO
    core = group % CORES
    x = x_hi * XLO + x_lo

    def device(xx, yy, zz, cc):
        return {"group": (yy * XLO + xx % XLO) * CORES + cc, "table": zz, "batch": xx // XLO}

    sibling = device(x, y, z, 1 - core)

    def x_peer(offset):
        return device((x + offset) % nx, y, z, core)

    def y_peer(offset):
        return device(x, (y + offset) % ny, z, core)

    def z_peer(offset):
        return device(x, y, (z + offset) % nz, core)

    def remote(src, dst, send, recv, target):
        return pltpu.make_async_remote_copy(
            src_ref=src, dst_ref=dst, send_sem=send, recv_sem=recv, device_id=target, device_id_type=MESH
        )

    def each(count, act):
        lax.fori_loop(0, count, lambda i, c: (act(i), c)[1], 0)

    def loads(k):
        cols = pl.ds(k * KCHUNK, KCHUNK)
        return (
            pltpu.make_async_copy(feat_hbm.at[:, cols], feat.at[:, cols], load_sem.at[0, k]),
            pltpu.make_async_copy(cot_hbm.at[:, cols], cot.at[:, cols], load_sem.at[1, k]),
            pltpu.make_async_copy(down_hbm.at[cols, :], down.at[cols, :], load_sem.at[2, k]),
            pltpu.make_async_copy(up_hbm.at[:, cols], up.at[:, cols], load_sem.at[3, k]),
        )

    for k in range(chunks):
        for copy in loads(k):
            copy.start()
    place = core * nx + x
    load_bias = pltpu.make_async_copy(bias_hbm, bias, load_sem.at[0, chunks])
    load_ids = pltpu.make_async_copy(ids_hbm, ids.at[place], load_sem.at[1, chunks])
    load_bias.start()
    load_ids.start()

    barrier = pltpu.get_barrier_semaphore()

    def greet(target):
        pl.semaphore_signal(barrier, inc=1, device_id=target, device_id_type=MESH)

    each(nz - 1, lambda i: greet(z_peer(offset_of(i, nz))))
    each(ny - 1, lambda i: greet(y_peer(offset_of(i, ny))))
    for offset in range(1, nx):
        greet(x_peer(offset))
        greet(device((x + offset) % nx, y, z, 1 - core))
    greet(sibling)

    acc[...] = jnp.zeros_like(acc)
    bias_part[...] = jnp.zeros_like(bias_part)

    for k in range(chunks):
        for copy in loads(k):
            copy.wait()
        cols = slice(k * KCHUNK, (k + 1) * KCHUNK)
        part_in = feat[:, cols]
        gate_grad = cot[:, cols].astype(F32) * part_in.astype(F32)
        sums = jnp.sum(gate_grad, 0, keepdims=True)
        for j in range(KCHUNK // 128):
            g = k * (KCHUNK // 128) + j
            bias_part[g // 2, g % 2 : g % 2 + 1, :] = sums[:, j * 128 : (j + 1) * 128]
        first = jnp.dot(part_in, down[cols, :], preferred_element_type=F32)
        second = lax.dot_general(
            gate_grad.astype(BF16), up[:, cols], (((1,), (1,)), ((), ())), preferred_element_type=F32
        )
        if k == 0:
            low_acc[...] = first
            grad_acc[...] = second
        else:
            low_acc[...] += first
            grad_acc[...] += second
    low[...] = low_acc[...].astype(BF16)
    low_grad[...] = grad_acc[...].astype(BF16)
    load_bias.wait()
    load_ids.wait()

    def columns(start, count):
        cols = slice(start, start + count)
        gate = jnp.dot(low[...], up[:, cols], preferred_element_type=F32) + bias[cols].reshape(1, count)
        back = lax.dot_general(
            low_grad[...], down[cols, :], (((1,), (1,)), ((), ())), preferred_element_type=F32
        )
        return (cot[:, cols].astype(F32) * (gate + 1.0) + back).astype(BF16)

    for f in range(0, nz, 2):
        pair = columns(128 + f * 128, 256)
        pooled[f] = pair[:, :128]
        pooled[f + 1] = pair[:, 128:]

    pl.semaphore_wait(barrier, (nz - 1) + (ny - 1) + 2 * (nx - 1) + 1)

    def bias_z_copy(step):
        offset = near_of(step, nz)
        return remote(
            bias_part.at[(z + offset) % nz], bias_z.at[z], bzs_sem.at[step], bzr_sem.at[z], z_peer(offset)
        )

    each(nz - 1, lambda s: bias_z_copy(s).start())

    mine = pl.ds(pl.multiple_of(x * 128, 128), 128)

    def z_copy(step):
        offset = near_of(step, nz)
        return remote(
            pooled.at[(z + offset) % nz], vals.at[z, core, mine], zs_sem.at[step], zr_sem.at[z], z_peer(offset)
        )

    each(nz - 1, lambda s: z_copy(s).start())

    def id_copy(i):
        if i == nx - 1:
            target = sibling
        elif i < nx - 1:
            target = x_peer(i + 1)
        else:
            target = device((x + i - nx + 1) % nx, y, z, 1 - core)
        return remote(ids.at[place], ids.at[place], id_sem.at[i], idr_sem.at[place], target)

    for i in range(2 * nx - 1):
        id_copy(i).start()

    vals[z, core, mine] = pooled[z]

    def source_of(step):
        return (z + nz - near_of(step, nz)) % nz

    def z_wait(source):
        remote(pooled.at[0], vals.at[source, core, mine], zs_sem.at[0], zr_sem.at[source], sibling).wait_recv()

    def x_copy(source, i):
        spot = vals.at[source, core, mine]
        return remote(spot, spot, xs_sem.at[source, i], xr_sem.at[source, x], x_peer(offset_of(i, nx)))

    def x_send(source):
        for i in range(nx - 1):
            x_copy(source, i).start()

    def x_wait(source):
        for i in range(nx - 1):
            there = (x + nx - offset_of(i, nx)) % nx
            spot = vals.at[source, core, pl.ds(pl.multiple_of(there * 128, 128), 128)]
            remote(spot, spot, xs_sem.at[source, i], xr_sem.at[source, there], sibling).wait_recv()

    def core_copy(source):
        spot = vals.at[source, core]
        return remote(spot, spot, fs_sem.at[source], fr_sem.at[source], sibling)

    def core_wait(source):
        spot = vals.at[source, 1 - core]
        remote(spot, spot, fs_sem.at[source], fr_sem.at[source], sibling).wait_recv()

    x_send(z)

    bottom_ref[...] = columns(0, 128)

    for c in range(CORES):
        for xx in range(nx):
            k = c * nx + xx

            @pl.when(k != place)
            def _():
                remote(ids.at[k], ids.at[k], id_sem.at[0], idr_sem.at[k], sibling).wait_recv()

            row = ids[k]
            block = row >> 7
            here = (((block >> 1) & 1) == core) & ((block & 1) == x_hi) & (((block >> 2) & 1) == x_lo)
            tile_of[2 * k : 2 * k + 2, :] = jnp.where(here, block >> 3, -1)
            inner[2 * k : 2 * k + 2, :] = row & 127

    def products(source, tiles):
        part = pl.ds(pl.multiple_of(source * 128, 128), 128)
        tile_here, inner_here = tile_of[:, part], inner[:, part]
        value = vals[source].reshape(CORES * nx * 128, EMB)
        rows = lax.broadcasted_iota(jnp.int32, (ROWS_DEV, 128), 0).astype(F32).astype(BF16)
        one, zero = jnp.ones((), BF16), jnp.zeros((), BF16)
        for t in tiles:
            hit = jnp.where(tile_here == t, inner_here, -1).astype(F32).astype(BF16)
            onehot = jnp.concatenate(
                [
                    jnp.where(rows == hit[2 * k : 2 * k + 1], one, zero)
                    + jnp.where(rows == hit[2 * k + 1 : 2 * k + 2], one, zero)
                    for k in range(CORES * nx)
                ],
                1,
            )
            yield t, jnp.dot(onehot, value, preferred_element_type=F32)

    def add_rows(source):
        for t, product in products(source, range(ny)):
            acc[t * 128 : (t + 1) * 128, :] += product

    def nth(k):
        return source_of((k + nz - 1) % nz)

    def arrive(k):
        z_wait(nth(k))
        x_send(nth(k))

    def gather(k):
        x_wait(nth(k))
        core_copy(nth(k)).start()

    def add(k):
        core_wait(nth(k))
        add_rows(nth(k))

    def all_three(k, carry):
        arrive(k)
        gather(k - XLAG)
        add(k - CLAG)
        return carry

    for k in range(1, CLAG):
        arrive(k)
        if k >= XLAG:
            gather(k - XLAG)

    lax.fori_loop(CLAG, CUTS[0], all_three, 0)

    def bias_z_wait(step):
        source = source_of(step)
        remote(bias_part.at[0], bias_z.at[source], bzs_sem.at[0], bzr_sem.at[source], sibling).wait_recv()

    each(nz - 1, bias_z_wait)
    bias_z[z] = bias_part[z]
    bias_c[core] = jnp.sum(bias_z[...], 0)
    c_copy = remote(bias_c.at[core], bias_c.at[core], bc_sem.at[0], bc_sem.at[1], sibling)
    c_copy.start()

    lax.fori_loop(CUTS[0], CUTS[1], all_three, 0)

    def bx_copy(i):
        return remote(bias_x.at[x], bias_x.at[x], bxs_sem.at[i], bxr_sem.at[x], x_peer(offset_of(i, nx)))

    def by_copy(j):
        return remote(bias_y.at[y], bias_y.at[y], bys_sem.at[j], byr_sem.at[y], y_peer(offset_of(j, ny)))

    def ba_copy(step):
        return remote(
            bias_all.at[z], bias_all.at[z], bas_sem.at[step], bar_sem.at[z], z_peer(near_of(step, nz))
        )

    remote(bias_c.at[core], bias_c.at[1 - core], bc_sem.at[0], bc_sem.at[1], sibling).wait_recv()
    bias_x[x] = bias_c[0] + bias_c[1]
    for i in range(nx - 1):
        bx_copy(i).start()

    lax.fori_loop(CUTS[1], CUTS[2], all_three, 0)

    for i in range(nx - 1):
        source = (x + nx - offset_of(i, nx)) % nx
        remote(bias_x.at[x], bias_x.at[source], bxs_sem.at[i], bxr_sem.at[source], sibling).wait_recv()
    bias_y[y] = jnp.sum(bias_x[...], 0)
    each(ny - 1, lambda j: by_copy(j).start())

    lax.fori_loop(CUTS[2], CUTS[3], all_three, 0)

    def by_wait(j):
        source = (y + ny - offset_of(j, ny)) % ny
        remote(bias_y.at[y], bias_y.at[source], bys_sem.at[j], byr_sem.at[source], sibling).wait_recv()

    each(ny - 1, by_wait)
    bias_all[z] = jnp.sum(bias_y[...], 0)
    each(nz - 1, lambda s: ba_copy(s).start())

    lax.fori_loop(CUTS[3], nz, all_three, 0)

    for k in range(nz, nz + CLAG - 1):
        if k - XLAG < nz:
            gather(k - XLAG)
        add(k - CLAG)
    last = nth(nz - 1)
    core_wait(last)

    def y_copy(j):
        return remote(ys.at[j], yr.at[j], ys_sem.at[j], yr_sem.at[j], y_peer(offset_of(j, ny)))

    order = [(y + offset_of(j, ny)) % ny for j in range(ny)]
    total = None
    for j, (t, product) in enumerate(products(last, order)):
        whole = acc[pl.ds(pl.multiple_of(t * 128, 128), 128), :] + product
        if j < ny - 1:
            ys[j] = whole.astype(BF16)
            y_copy(j).start()
        else:
            total = whole

    for i in range(2 * nx - 1):
        id_copy(i).wait_send()
    c_copy.wait_send()
    for i in range(nx - 1):
        bx_copy(i).wait_send()
    each(ny - 1, lambda j: by_copy(j).wait_send())

    def sent_z(step):
        z_copy(step).wait_send()
        bias_z_copy(step).wait_send()

    def sent_block(source):
        for i in range(nx - 1):
            x_copy(source, i).wait_send()
        core_copy(source).wait_send()

    each(nz - 1, sent_z)
    each(nz, sent_block)

    def ba_wait(step):
        source = source_of(step)
        remote(bias_all.at[z], bias_all.at[source], bas_sem.at[0], bar_sem.at[source], sibling).wait_recv()
        ba_copy(step).wait_send()

    each(nz - 1, ba_wait)
    for g in range(width // 128):
        bias_out[g : g + 1, :] = bias_all[g // 2, g % 2 : g % 2 + 1, :]

    for j in range(ny - 1):
        y_copy(j).wait_recv()
        total += yr[j].astype(F32)
    row_out[...] = total
    each(ny - 1, lambda j: y_copy(j).wait_send())


def body(sizes, features_in, cross_cot, cross_down, cross_up, cross_bias, lookups):
    ny, nx, nz = sizes
    samples, width = features_in.shape[1:]
    rank = cross_down.shape[1]
    tsamp = lookups.shape[2]
    group = CORES * nx
    vmem = pl.BlockSpec(memory_space=pltpu.VMEM)
    anywhere = pl.BlockSpec(memory_space=pl.ANY)
    dma = pltpu.SemaphoreType.DMA
    bottom, bias, rows = pl.pallas_call(
        functools.partial(kernel, sizes),
        out_shape=(
            jax.ShapeDtypeStruct((samples, EMB), BF16),
            jax.ShapeDtypeStruct((width // 128, 128), F32),
            jax.ShapeDtypeStruct((ROWS_DEV, EMB), F32),
        ),
        in_specs=[anywhere] * 6,
        out_specs=(vmem, vmem, vmem),
        scratch_shapes=[
            pltpu.VMEM((samples, width), BF16),
            pltpu.VMEM((samples, width), BF16),
            pltpu.VMEM((width, rank), BF16),
            pltpu.VMEM((rank, width), BF16),
            pltpu.VMEM((width,), F32),
            pltpu.VMEM((samples, rank), BF16),
            pltpu.VMEM((samples, rank), BF16),
            pltpu.VMEM((samples, rank), F32),
            pltpu.VMEM((samples, rank), F32),
            pltpu.VMEM((nz, samples, EMB), BF16),
            pltpu.VMEM((nz, CORES, nx * samples, EMB), BF16),
            pltpu.VMEM((group, 2, tsamp), jnp.int32),
            pltpu.VMEM((2 * group, tsamp), jnp.int32),
            pltpu.VMEM((2 * group, tsamp), jnp.int32),
            pltpu.VMEM((ny * ROWS_DEV, EMB), F32),
            pltpu.VMEM((ny - 1, ROWS_DEV, EMB), BF16),
            pltpu.VMEM((ny - 1, ROWS_DEV, EMB), BF16),
            pltpu.VMEM((nz, 2, 128), F32),
            pltpu.VMEM((nz, 2, 128), F32),
            pltpu.VMEM((CORES, 2, 128), F32),
            pltpu.VMEM((nx, 2, 128), F32),
            pltpu.VMEM((ny, 2, 128), F32),
            pltpu.VMEM((nz, 2, 128), F32),
            dma((4, width // KCHUNK + 1)),
            dma((2 * nx - 1,)),
            dma((2 * nx,)),
            dma((nz - 1,)),
            dma((nz,)),
            dma((nz, nx - 1)),
            dma((nz, nx)),
            dma((nz,)),
            dma((nz,)),
            dma((ny - 1,)),
            dma((ny - 1,)),
            dma((nz - 1,)),
            dma((nz,)),
            dma((2,)),
            dma((nx - 1,)),
            dma((nx,)),
            dma((ny - 1,)),
            dma((ny,)),
            dma((nz - 1,)),
            dma((nz,)),
        ],
        compiler_params=pltpu.CompilerParams(
            collective_id=0, has_side_effects=True, vmem_limit_bytes=53 << 20
        ),
        name="cross_backward",
    )(
        features_in[0],
        cross_cot[0],
        cross_down,
        cross_up,
        cross_bias,
        lookups[0, 0].T,
    )
    return bottom[None], bias.reshape(width), rows[None]


def solution(mesh):
    sizes = (
        mesh.shape["group"] // (XLO * CORES),
        XLO * mesh.shape["batch"],
        mesh.shape["table"],
    )
    placed = (
        P(("group", "batch"), "table", None),
        P(("group", "batch"), "table", None),
        P(),
        P(),
        P(),
        P("table", ("group", "batch"), None, None),
    )
    return jax.shard_map(
        functools.partial(body, sizes),
        mesh=mesh,
        in_specs=placed,
        out_specs=(P(("group", "batch"), "table", None), P(), P("table", ("group", "batch"), None)),
        check_vma=False,
    )
```
